512 devices in a mesh: band: 64 (over z, y_hi, core), tslice: 8 (over x, y_lo).
Axes of the slice: x: 4, y: 4 (y_hi: 2, y_lo: 2; y = y_hi * 2 + y_lo), z: 16, core: 2. Of those that a mesh axis runs over, the one named last changes fastest.
Arguments:
- voltages: bfloat16 [2048, 131072], P('band', 'tslice'), may hold values from -6 to 6
- taper: float32 [4, 2048], replicated, may hold values from -0.0625 to 0.0625
- input_of: int32 [2048], replicated, may hold values from 0 to 2047, each once
- band_start: int32 [64], replicated, may hold values from 0 to 4
Outputs:
- visibility: bfloat16 [64, 2, 2048, 2048], P('band', None, 'tslice')
The draws below stay inside these ranges and needn't reach their ends.
Inputs may be any that keep to these rules, and one draw needn't show every extreme that they name: `input_of`: every signal has its own input. `band_start`: a band's 12 correlated channels lie within its own 16 channels.
All inputs are finite; a program needn't handle non-finite values.
Results may differ from the reference program's by a relative error of at most 0.0069.
Values may be sent and summed in bfloat16 or wider, within the bound.
No kernel may reach another device: no remote copies, remote signals or barrier semaphores. Data moves between devices by JAX's collectives and lax.ppermute only.
A program may use at most 128 MiB of HBM per device.

```python
import jax
import jax.numpy as jnp
from jax import lax

SIGNALS = 2048
CHANNELS = 1024
TAPS = 4
CORR = 12
L = 2048
BANDS = 64
CH_BAND = 16
SAMPLES = 131072


def set_ends(array, key, least, high):
    extent = array.shape
    index_at = [jax.random.randint(jax.random.fold_in(key, axis), (), 0, extent[axis]) for axis in range(len(extent))]
    array = array.at[tuple(index_at)].set(least)
    longest = extent.index(max(extent))
    index_at[longest] = (index_at[longest] + 1) % extent[longest]
    return array.at[tuple(index_at)].set(high)


def level_of(rng, extent, cuts, smallest, largest):
    loudness = 1.0
    for axis_at, blocks in cuts:
        heights = jax.random.uniform(jax.random.fold_in(jax.random.fold_in(rng, 6), axis_at), (blocks,), jnp.float32, smallest / len(cuts), largest / len(cuts))
        loudness = loudness * jnp.repeat(jnp.exp(heights), extent[axis_at] // blocks).reshape((-1,) + (1,) * (len(extent) - 1 - axis_at))
    return loudness


def normal_values(own_key, shape, spread, most, shards=(), held_as=jnp.bfloat16):
    array = jax.random.normal(own_key, shape, jnp.float32) * spread
    if len(shards) > 0:
        array = level_of(own_key, shape, shards, -0.22, 0.18) * array
    return jnp.clip(array, min=-most, max=most).astype(held_as)


def setup_inputs(seed: int = 0) -> dict:
    key_list = jax.random.split(jax.random.key(seed), 5)
    voltages = normal_values(key_list[0], (SIGNALS, SAMPLES), 1.0, 6.0, ((0, 64), (1, 8)))
    taper = normal_values(key_list[1], (TAPS, L), (TAPS * L) ** -0.5, 0.0625, (), jnp.float32)
    input_of = jax.random.permutation(key_list[2], SIGNALS).astype(jnp.int32)
    band_start = set_ends(jax.random.randint(key_list[3], (BANDS,), 0, CH_BAND - CORR + 1), jax.random.fold_in(key_list[3], 1), 0, CH_BAND - CORR).astype(jnp.int32)
    return dict(voltages=voltages, taper=taper, input_of=input_of, band_start=band_start)


def make_basis(channel_ids, length):
    index = jnp.arange(length, dtype=jnp.int32)
    m = (channel_ids[:, None] * index[None, :]) % length
    phases = (2.0 * jnp.pi / length) * m.astype(jnp.float32)
    stacked = jnp.stack([jnp.cos(phases), -jnp.sin(phases)], axis=1)
    return stacked.reshape(2 * channel_ids.shape[0], length).astype(jnp.bfloat16)


def reference(voltages, taper, input_of, band_start):
    sig_count = voltages.shape[0]
    length = 2 * CHANNELS
    frames = voltages.shape[1] // length
    padded = jnp.concatenate([jnp.zeros((sig_count, (TAPS - 1) * length), jnp.float32), voltages.astype(jnp.float32)], axis=1)
    padded = padded.reshape(sig_count, frames + TAPS - 1, length)
    filtered = taper[0][None, None, :] * padded[:, 0:frames, :]
    for tap_index in range(1, TAPS):
        filtered = filtered + taper[tap_index][None, None, :] * padded[:, tap_index:tap_index + frames, :]
    filtered = filtered.astype(jnp.bfloat16).reshape(sig_count * frames, length)
    picked = (jnp.arange(BANDS, dtype=jnp.int32) * CH_BAND + band_start)[:, None] + jnp.arange(CORR, dtype=jnp.int32)[None, :]
    picked = picked.reshape(BANDS * CORR).astype(jnp.int32)
    basis = make_basis(picked, length)
    spectra = jnp.dot(basis, filtered.T, preferred_element_type=jnp.float32).astype(jnp.bfloat16)
    spectra = spectra.reshape(BANDS, CORR, 2, sig_count, frames)
    spectra = jnp.take(spectra, input_of, axis=3)
    norm_scale = 1.0 / (CORR * frames)

    def one_band(band_data):
        values = band_data.astype(jnp.float32)
        real_part = values[:, 0]
        imag_part = values[:, 1]
        vis_real = jnp.einsum("cjsf,cjtf->st", values, values)
        vis_imag = jnp.einsum("csf,ctf->st", imag_part, real_part) - jnp.einsum("csf,ctf->st", real_part, imag_part)
        return (jnp.stack([vis_real, vis_imag], axis=0) * norm_scale).astype(jnp.bfloat16)

    return lax.map(one_band, spectra)
```

```python
import functools

import jax
import jax.numpy as jnp
import numpy as np
from jax import lax
from jax.experimental import pallas as pl
from jax.experimental.pallas import tpu as pltpu
from jax.sharding import PartitionSpec as P

CHANNELS = 1024
TAPS = 4
CORR = 12
MIB = 1 << 20
NT = (((1,), (1,)), ((), ()))


def make_basis(bands, length):
    index = np.arange(length, dtype=np.int64)
    m = (np.arange(CHANNELS, dtype=np.int64)[:, None] * index[None, :]) % length
    phases = np.float32(2.0 * np.pi / length) * m.astype(np.float32)
    stacked = np.stack([np.cos(phases), -np.sin(phases)], axis=0)
    stacked = stacked.reshape(2, bands, CHANNELS // bands, length).transpose(1, 0, 2, 3)
    return stacked.reshape(2 * CHANNELS, length).astype(jnp.bfloat16)


def spectra_kernel(group, start_ref, volt_ref, before_ref, taper_ref, basis_ref, out_ref, filt):
    sig_dev = volt_ref.shape[0]
    length = taper_ref.shape[1]
    frames = volt_ref.shape[1] // length
    ch_band = basis_ref.shape[0] // (2 * group)
    step = pl.program_id(0)

    @pl.when(step == 0)
    def _():
        def frame(at):
            if at < 0:
                return before_ref[:, (at + TAPS - 1) * length : (at + TAPS) * length]
            return volt_ref[:, at * length : (at + 1) * length]

        for at in range(frames):
            total = taper_ref[0:1, :] * frame(at - TAPS + 1).astype(jnp.float32)
            for tap in range(1, TAPS):
                total = total + taper_ref[tap : tap + 1, :] * frame(
                    at + tap - TAPS + 1
                ).astype(jnp.float32)
            filt[at * sig_dev : (at + 1) * sig_dev, :] = total.astype(jnp.bfloat16)

    products = lax.dot_general(
        basis_ref[...], filt[...], NT, preferred_element_type=jnp.float32
    ).astype(jnp.bfloat16)
    shape = (2 * CORR, products.shape[0])
    row = lax.broadcasted_iota(jnp.int32, shape, 0)
    at_first = lax.broadcasted_iota(jnp.int32, shape, 1) - row
    at_first = at_first - jnp.where(row < CORR, 0, ch_band - CORR)
    picks = [
        jnp.where(at_first == band * 2 * ch_band + start_ref[step * group + band], 1.0, 0.0)
        for band in range(group)
    ]
    picked = jnp.concatenate(picks, axis=0).astype(jnp.bfloat16)
    spectra = jnp.dot(picked, products, preferred_element_type=jnp.float32)
    for band in range(group):
        out_ref[band] = spectra[band * 2 * CORR : (band + 1) * 2 * CORR].astype(jnp.bfloat16)


def picked_spectra(voltages, before, taper, basis, band_start, bands):
    group = 8
    sig_dev, samples = voltages.shape
    length = taper.shape[1]
    columns = sig_dev * (samples // length)
    rows = 2 * CHANNELS // bands * group
    return pl.pallas_call(
        functools.partial(spectra_kernel, group),
        grid_spec=pltpu.PrefetchScalarGridSpec(
            num_scalar_prefetch=1,
            grid=(bands // group,),
            in_specs=[
                pl.BlockSpec(voltages.shape, lambda g, s: (0, 0)),
                pl.BlockSpec(before.shape, lambda g, s: (0, 0)),
                pl.BlockSpec(taper.shape, lambda g, s: (0, 0)),
                pl.BlockSpec((rows, length), lambda g, s: (g, 0)),
            ],
            out_specs=pl.BlockSpec((group, 2 * CORR, columns), lambda g, s: (g, 0, 0)),
            scratch_shapes=[
                pltpu.VMEM((columns, length), jnp.bfloat16),
            ],
        ),
        out_shape=jax.ShapeDtypeStruct((bands, 2 * CORR, columns), jnp.bfloat16),
        compiler_params=pltpu.CompilerParams(vmem_limit_bytes=40 * MIB),
        cost_estimate=pl.CostEstimate(
            flops=2 * 2 * CHANNELS * length * columns,
            bytes_accessed=2 * 2 * CHANNELS * length + 4 * sig_dev * samples,
            transcendentals=0,
        ),
    )(band_start, voltages, before, taper, basis)


def order_kernel(turned_ref, input_ref, out_ref, lined):
    bands, values, columns = turned_ref.shape
    signals = out_ref.shape[1]
    sig_dev = signals // bands
    frames = columns // sig_dev
    per_tile = 128 // sig_dev

    def tile(at, carry):
        lane = lax.broadcasted_iota(jnp.int32, (values, 128), 1) // sig_dev
        blocks = [turned_ref[at * per_tile + k].astype(jnp.float32) for k in range(per_tile)]
        for frame in range(frames):
            half, place = frame // per_tile, frame % per_tile
            merged = None
            for k in range(per_tile):
                piece = blocks[k][:, half * 128 : (half + 1) * 128]
                shift = (k - place) * sig_dev % 128
                if shift:
                    piece = pltpu.roll(piece, shift, 1)
                merged = piece if merged is None else jnp.where(lane == k, piece, merged)
            lined[at, frame * values : (frame + 1) * values, :] = merged
        return carry

    lax.fori_loop(0, bands // per_tile, tile, 0)
    wanted = input_ref[...]
    part = 256
    total = None
    for at in range(signals // part):
        held = jnp.concatenate([lined[2 * at], lined[2 * at + 1]], axis=1).astype(jnp.bfloat16)
        row = lax.broadcasted_iota(jnp.int32, (part, signals), 0) + at * part
        chosen = jnp.where(row == wanted, 1.0, 0.0).astype(jnp.bfloat16)
        product = jnp.dot(held, chosen, preferred_element_type=jnp.float32)
        total = product if total is None else total + product
    out_ref[...] = total.astype(jnp.bfloat16)


def order_signals(turned, input_of):
    bands, values, columns = turned.shape
    signals = input_of.shape[0]
    rows = values * columns * bands // signals
    return pl.pallas_call(
        order_kernel,
        in_specs=[pl.BlockSpec(memory_space=pltpu.VMEM)] * 2,
        out_specs=pl.BlockSpec(memory_space=pltpu.VMEM),
        out_shape=jax.ShapeDtypeStruct((rows, signals), jnp.bfloat16),
        scratch_shapes=[pltpu.VMEM((signals // 128, rows, 128), jnp.float32)],
        compiler_params=pltpu.CompilerParams(vmem_limit_bytes=40 * MIB),
        cost_estimate=pl.CostEstimate(
            flops=2 * rows * signals * signals,
            bytes_accessed=4 * rows * signals,
            transcendentals=0,
        ),
    )(turned, input_of.reshape(1, signals))


def correlate_kernel(scale, count, position_ref, *refs):
    own_refs, tile_refs = refs[:count], refs[count : 2 * count]
    out_ref, left = refs[2 * count], refs[2 * count + 1]
    row_count = out_ref.shape[2]
    values = 2 * CORR

    @pl.when(pl.program_id(0) == 0)
    def _():
        own = jnp.concatenate([r[...] for r in own_refs], axis=0)
        depth = own.shape[0]
        part = 384
        row = lax.broadcasted_iota(jnp.int32, (part, part), 0)
        column = lax.broadcasted_iota(jnp.int32, (part, part), 1)
        upper = row % values < CORR
        swap = jnp.where(upper & (column == row + CORR), 1.0, 0.0)
        swap = swap - jnp.where(jnp.logical_not(upper) & (column == row - CORR), 1.0, 0.0)
        swap = swap.astype(jnp.bfloat16)
        for at in range(depth // part):
            piece = own[at * part : (at + 1) * part]
            left[:row_count, at * part : (at + 1) * part] = jnp.transpose(
                piece.astype(jnp.float32)
            ).astype(jnp.bfloat16)
            turned = jnp.dot(swap, piece, preferred_element_type=jnp.float32)
            left[row_count:, at * part : (at + 1) * part] = jnp.transpose(turned).astype(
                jnp.bfloat16
            )

    right = jnp.concatenate([r[...] for r in tile_refs], axis=0)
    summed = jnp.dot(left[...], right, preferred_element_type=jnp.float32) * scale
    out_ref[0, 0] = summed[:row_count].astype(jnp.bfloat16)
    out_ref[0, 1] = summed[row_count:].astype(jnp.bfloat16)


def correlate(position, blocks, row_count, scale):
    signals = blocks[0].shape[1]
    depth = sum(b.shape[0] for b in blocks)
    tile = 512
    count = len(blocks)
    own_specs = [pl.BlockSpec((b.shape[0], row_count), lambda g, p: (0, p[0])) for b in blocks]
    tile_specs = [pl.BlockSpec((b.shape[0], tile), lambda g, p: (0, g)) for b in blocks]
    return pl.pallas_call(
        functools.partial(correlate_kernel, scale, count),
        grid_spec=pltpu.PrefetchScalarGridSpec(
            num_scalar_prefetch=1,
            grid=(signals // tile,),
            in_specs=own_specs + tile_specs,
            out_specs=pl.BlockSpec((1, 2, row_count, tile), lambda g, p: (0, 0, 0, g)),
            scratch_shapes=[pltpu.VMEM((2 * row_count, depth), jnp.bfloat16)],
        ),
        out_shape=jax.ShapeDtypeStruct((1, 2, row_count, signals), jnp.bfloat16),
        compiler_params=pltpu.CompilerParams(vmem_limit_bytes=40 * MIB),
        cost_estimate=pl.CostEstimate(
            flops=4 * row_count * signals * depth,
            bytes_accessed=2 * signals * depth + 4 * row_count * signals,
            transcendentals=0,
        ),
    )(position, *blocks, *blocks)


def from_slice(value, dx, dy, slices):
    along = slices // 2
    pairs = []
    for target in range(slices):
        source = ((target // 2 + dx) % along) * 2 + (target % 2 + dy) % 2
        pairs.append((source, target))
    return lax.ppermute(value, "tslice", pairs)


def gather_slices(own, slices):
    take = functools.partial(from_slice, slices=slices)
    right = take(own, 1, 0)
    other = take(own, 0, 1)
    left = take(own, -1, 0)
    right_other = take(right, 0, 1)
    left_other = take(other, -1, 0)
    far = take(right, 1, 0)
    third = own.shape[0] // 3
    far_other = [
        take(right_other[:third], 1, 0),
        take(left_other[third : 2 * third], -1, 0),
        take(far[2 * third :], 0, 1),
    ]
    return [own, right, other, left, right_other, left_other, far] + far_other


def on_device(voltages, taper, input_of, band_start):
    length = 2 * CHANNELS
    bands = lax.axis_size("band")
    slices = lax.axis_size("tslice")
    frames = voltages.shape[1] // length
    signals = input_of.shape[0]
    position = lax.axis_index("tslice")
    tail = voltages[:, (frames - TAPS + 1) * length :]
    before = lax.ppermute(tail, "tslice", [(s, s + 1) for s in range(slices - 1)])
    basis = jnp.asarray(make_basis(bands, length))
    spectra = picked_spectra(voltages, before, taper, basis, band_start, bands)
    turned = lax.all_to_all(spectra, "band", split_axis=0, concat_axis=0, tiled=True)
    own = order_signals(turned, input_of)
    blocks = gather_slices(own, slices)
    scale = 1.0 / (CORR * frames * slices)
    return correlate(
        position.astype(jnp.int32).reshape(1), blocks, signals // slices, scale
    )


def solution(mesh):
    return jax.shard_map(
        on_device,
        mesh=mesh,
        in_specs=(P("band", "tslice"), P(), P(), P()),
        out_specs=P("band", None, "tslice", None),
        check_vma=False,
    )
```

```python
import functools

import jax
import jax.numpy as jnp
import numpy as np
from jax import lax
from jax.experimental import pallas as pl
from jax.experimental.pallas import tpu as pltpu
from jax.sharding import PartitionSpec as P

CHANNELS = 1024
TAPS = 4
CORR = 12
VMEM_LIMIT = 32 << 20
NT = (((1,), (1,)), ((), ()))


def make_basis(bands, length):
    index = np.arange(length, dtype=np.int64)
    m = (np.arange(CHANNELS, dtype=np.int64)[:, None] * index[None, :]) % length
    phases = np.float32(2.0 * np.pi / length) * m.astype(np.float32)
    stacked = np.stack([np.cos(phases), -np.sin(phases)], axis=0)
    stacked = stacked.reshape(2, bands, CHANNELS // bands, length).transpose(1, 0, 2, 3)
    return stacked.reshape(2 * CHANNELS, length).astype(jnp.bfloat16)


def spectra_kernel(group, span, start_ref, volt_ref, before_ref, taper_ref, basis_ref, *refs):
    out_ref, filt = refs[-2:]
    sig_dev = volt_ref.shape[0]
    length = taper_ref.shape[1]
    bands = out_ref.shape[0]
    ch_band = basis_ref.shape[0] // (2 * bands)
    held = group * 2 * ch_band

    def frame(at):
        if at < 0:
            return before_ref[:, (at + TAPS - 1) * length : (at + TAPS) * length]
        return volt_ref[:, at * length : (at + 1) * length]

    totals = []
    for at in span:
        total = taper_ref[0:1, :] * frame(at - TAPS + 1).astype(jnp.float32)
        for tap in range(1, TAPS):
            total = total + taper_ref[tap : tap + 1, :] * frame(at + tap - TAPS + 1).astype(
                jnp.float32
            )
        totals.append(total)
    filt[...] = jnp.transpose(jnp.concatenate(totals, axis=0)).astype(jnp.bfloat16)

    part = 8
    shape = (2 * CORR, part * 2 * ch_band)
    row = lax.broadcasted_iota(jnp.int32, shape, 0)
    at_first = lax.broadcasted_iota(jnp.int32, shape, 1) - row
    at_first = at_first - jnp.where(row < CORR, 0, ch_band - CORR)

    def bands_from(at, carry):
        first = pl.multiple_of(at * held, held)
        products = jnp.dot(
            basis_ref[pl.ds(first, held), :], filt[...], preferred_element_type=jnp.float32
        ).astype(jnp.bfloat16)
        for begin in range(0, group, part):
            band_at = at * group + begin
            picks = [
                jnp.where(at_first == band * 2 * ch_band + start_ref[band_at + band], 1.0, 0.0)
                for band in range(part)
            ]
            spectra = jnp.dot(
                jnp.concatenate(picks, axis=0).astype(jnp.bfloat16),
                products[begin * 2 * ch_band : (begin + part) * 2 * ch_band],
                preferred_element_type=jnp.float32,
            )
            for band in range(part):
                these = spectra[band * 2 * CORR : (band + 1) * 2 * CORR].astype(jnp.bfloat16)
                if len(refs) == 3:
                    these = jnp.concatenate([these, refs[0][band_at + band]], axis=1)
                out_ref[band_at + band] = these
        return carry

    lax.fori_loop(0, bands // group, bands_from, 0)


def picked_spectra(voltages, before, taper, basis, band_start, bands, span, later=None):
    sig_dev, samples = voltages.shape
    length = taper.shape[1]
    columns = sig_dev * len(span)
    wide = columns if later is None else columns + later.shape[2]
    beside = [] if later is None else [later]
    whole = pl.BlockSpec(memory_space=pltpu.VMEM)
    return pl.pallas_call(
        functools.partial(spectra_kernel, 16, span),
        in_specs=[pl.BlockSpec(memory_space=pltpu.SMEM)] + [whole] * (4 + len(beside)),
        out_specs=whole,
        scratch_shapes=[pltpu.VMEM((length, columns), jnp.bfloat16)],
        out_shape=jax.ShapeDtypeStruct((bands, 2 * CORR, wide), jnp.bfloat16),
        compiler_params=pltpu.CompilerParams(vmem_limit_bytes=VMEM_LIMIT),
        cost_estimate=pl.CostEstimate(
            flops=2 * 2 * CHANNELS * length * columns,
            bytes_accessed=2 * 2 * CHANNELS * length + 4 * sig_dev * samples,
            transcendentals=0,
        ),
    )(band_start, voltages, before, taper, basis, *beside)


def order_kernel(turned_ref, input_ref, out_ref, lined):
    bands, values, columns = turned_ref.shape
    signals = out_ref.shape[1]
    sig_dev = signals // bands
    frames = columns // sig_dev
    per_tile = 128 // sig_dev

    def tile(at, carry):
        lane = lax.broadcasted_iota(jnp.int32, (values, 128), 1) // sig_dev
        blocks = [turned_ref[at * per_tile + k].astype(jnp.float32) for k in range(per_tile)]
        for frame in range(frames):
            half, place = frame // per_tile, frame % per_tile
            merged = None
            for k in range(per_tile):
                piece = blocks[k][:, half * 128 : (half + 1) * 128]
                shift = (k - place) * sig_dev % 128
                if shift:
                    piece = pltpu.roll(piece, shift, 1)
                merged = piece if merged is None else jnp.where(lane == k, piece, merged)
            lined[at, frame * values : (frame + 1) * values, :] = merged
        return carry

    lax.fori_loop(0, bands // per_tile, tile, 0)
    wanted = jnp.broadcast_to(input_ref[...], (16, signals)).astype(jnp.int16)
    row = lax.broadcasted_iota(jnp.int32, (16, signals), 0).astype(jnp.int16)
    one = jnp.ones((16, signals), jnp.bfloat16)
    zero = jnp.zeros((16, signals), jnp.bfloat16)
    part = 256
    total = None
    for at in range(signals // part):
        held = jnp.concatenate([lined[2 * at], lined[2 * at + 1]], axis=1).astype(jnp.bfloat16)
        chosen = jnp.concatenate(
            [
                jnp.where(row == wanted - (at * part + first), one, zero)
                for first in range(0, part, 16)
            ],
            axis=0,
        )
        product = jnp.dot(held, chosen, preferred_element_type=jnp.float32)
        total = product if total is None else total + product
    out_ref[...] = total.astype(jnp.bfloat16)


def order_signals(turned, input_of):
    bands, values, columns = turned.shape
    signals = input_of.shape[0]
    rows = values * columns * bands // signals
    return pl.pallas_call(
        order_kernel,
        in_specs=[pl.BlockSpec(memory_space=pltpu.VMEM)] * 2,
        out_specs=pl.BlockSpec(memory_space=pltpu.VMEM),
        out_shape=jax.ShapeDtypeStruct((rows, signals), jnp.bfloat16),
        scratch_shapes=[pltpu.VMEM((signals // 128, rows, 128), jnp.float32)],
        compiler_params=pltpu.CompilerParams(vmem_limit_bytes=VMEM_LIMIT),
        cost_estimate=pl.CostEstimate(
            flops=2 * rows * signals * signals,
            bytes_accessed=4 * rows * signals,
            transcendentals=0,
        ),
    )(turned, input_of.reshape(1, signals))


def correlate_kernel(scale, count, tile, position_ref, *refs):
    blocks, before, out_ref, left = refs[:count], refs[count:-2], refs[-2], refs[-1]
    row_count = left.shape[0] // 2
    values = 2 * CORR
    step = pl.program_id(0)

    @pl.when(step == 0)
    def _():
        first = pl.multiple_of(position_ref[0] * row_count, row_count)
        own = jnp.concatenate([r[:, pl.ds(first, row_count)] for r in blocks], axis=0)
        part = 192
        row = lax.broadcasted_iota(jnp.int32, (part, part), 0)
        column = lax.broadcasted_iota(jnp.int32, (part, part), 1)
        upper = row % values < CORR
        swap = jnp.where(upper & (column == row + CORR), 1.0, 0.0)
        swap = swap - jnp.where(jnp.logical_not(upper) & (column == row - CORR), 1.0, 0.0)
        swap = swap.astype(jnp.bfloat16)
        pieces = [own[at : at + part] for at in range(0, own.shape[0], part)]
        turned = [jnp.dot(swap, p, preferred_element_type=jnp.float32) for p in pieces]
        left[:row_count] = jnp.transpose(own.astype(jnp.float32)).astype(jnp.bfloat16)
        left[row_count:] = jnp.transpose(jnp.concatenate(turned, axis=0)).astype(jnp.bfloat16)

    columns = pl.ds(pl.multiple_of(step * tile, tile), tile)
    right = jnp.concatenate([r[:, columns] for r in blocks], axis=0)
    summed = jnp.dot(left[...], right, preferred_element_type=jnp.float32)
    if before:
        summed = summed + before[0][:, columns]
    if scale is None:
        out_ref[:, columns] = summed
    else:
        summed = summed * scale
        out_ref[0, 0] = summed[:row_count].astype(jnp.bfloat16)
        out_ref[0, 1] = summed[row_count:].astype(jnp.bfloat16)


def correlate(position, blocks, row_count, before=(), scale=None):
    signals = blocks[0].shape[1]
    depth = sum(b.shape[0] for b in blocks)
    tile = 512
    whole = pl.BlockSpec(memory_space=pltpu.VMEM)
    if scale is None:
        out_spec = whole
        out_shape = jax.ShapeDtypeStruct((2 * row_count, signals), jnp.float32)
    else:
        out_spec = pl.BlockSpec((1, 2, row_count, tile), lambda g, p: (0, 0, 0, g))
        out_shape = jax.ShapeDtypeStruct((1, 2, row_count, signals), jnp.bfloat16)
    return pl.pallas_call(
        functools.partial(correlate_kernel, scale, len(blocks), tile),
        grid_spec=pltpu.PrefetchScalarGridSpec(
            num_scalar_prefetch=1,
            grid=(signals // tile,),
            in_specs=[whole] * (len(blocks) + len(before)),
            out_specs=out_spec,
            scratch_shapes=[pltpu.VMEM((2 * row_count, depth), jnp.bfloat16)],
        ),
        out_shape=out_shape,
        compiler_params=pltpu.CompilerParams(vmem_limit_bytes=VMEM_LIMIT),
        cost_estimate=pl.CostEstimate(
            flops=4 * row_count * signals * depth,
            bytes_accessed=2 * signals * depth + 8 * row_count * signals,
            transcendentals=0,
        ),
    )(position, *blocks, *before)


def from_slice(value, dx, dy, slices):
    along = slices // 2
    pairs = []
    for target in range(slices):
        source = ((target // 2 + dx) % along) * 2 + (target % 2 + dy) % 2
        pairs.append((source, target))
    return lax.ppermute(value, "tslice", pairs)


def gather_and_correlate(own, position, slices, row_count, scale):
    take = functools.partial(from_slice, slices=slices)
    near = lax.optimization_barrier((take(own, 1, 0), take(own, 0, 1), take(own, -1, 0)))
    right, other, left = near
    summed = correlate(position, [own, right, other, left], row_count)
    right_other, left_other, far = take(right, 0, 1), take(other, -1, 0), take(right, 1, 0)
    left_other, summed = lax.optimization_barrier((left_other, summed))
    third = own.shape[0] // 3
    last = [
        take(right_other[:third], 1, 0),
        take(left_other[third : 2 * third], -1, 0),
        take(far[2 * third :], 0, 1),
    ]
    summed = correlate(position, [right_other, left_other, far], row_count, [summed])
    return correlate(position, last, row_count, [summed], scale)


def on_device(voltages, taper, input_of, band_start):
    length = 2 * CHANNELS
    bands = lax.axis_size("band")
    slices = lax.axis_size("tslice")
    frames = voltages.shape[1] // length
    signals = input_of.shape[0]
    position = lax.axis_index("tslice")
    tail = voltages[:, (frames - TAPS + 1) * length :]
    before = lax.ppermute(tail, "tslice", [(s, s + 1) for s in range(slices - 1)])
    basis = jnp.asarray(make_basis(bands, length))
    half = frames // 2
    transform = functools.partial(picked_spectra, voltages)
    rest = (taper, basis, band_start, bands)
    later = transform(voltages[:8, :128], *rest, tuple(range(half, frames)))
    spectra = transform(before, *rest, tuple(range(half)), later)
    turned = lax.all_to_all(spectra, "band", split_axis=0, concat_axis=0, tiled=True)
    own = order_signals(turned, input_of)
    position = position.astype(jnp.int32).reshape(1)
    scale = 1.0 / (CORR * frames * slices)
    return gather_and_correlate(own, position, slices, signals // slices, scale)


def solution(mesh):
    return jax.shard_map(
        on_device,
        mesh=mesh,
        in_specs=(P("band", "tslice"), P(), P(), P()),
        out_specs=P("band", None, "tslice", None),
        check_vma=False,
    )
```

```python
import functools

import jax
import jax.numpy as jnp
import numpy as np
from jax import lax
from jax.experimental import pallas as pl
from jax.experimental.pallas import tpu as pltpu
from jax.sharding import PartitionSpec as P

CHANNELS = 1024
TAPS = 4
CORR = 12
VMEM_LIMIT = 16 << 20


def make_basis(bands, length):
    half = length // 2
    index = np.arange(half, dtype=np.int64)
    m = (np.arange(CHANNELS, dtype=np.int64)[:, None] * index[None, :]) % length
    phases = np.float32(2.0 * np.pi / length) * m.astype(np.float32)
    stacked = np.stack([np.cos(phases), -np.sin(phases)], axis=0)
    stacked = stacked.reshape(2, bands, CHANNELS // bands // 2, 2, half)
    stacked = stacked.transpose(3, 1, 0, 2, 4).reshape(2, CHANNELS, half)
    return stacked.astype(jnp.bfloat16)


def spectra_kernel(group, span, start_ref, volt_ref, taper_ref, basis_ref, *refs):
    out_ref, folded = refs[-2:]
    before_ref, later_ref = refs[:2] if len(refs) == 4 else (None, None)
    sig_dev = volt_ref.shape[0]
    length = taper_ref.shape[1]
    half = length // 2
    bands = out_ref.shape[0]
    columns = sig_dev * len(span)
    ch_band = basis_ref.shape[1] // bands

    def frame(at, second):
        first = second * half
        if at < 0:
            first = first + (at + TAPS - 1) * length
            return before_ref[:, first : first + half].astype(jnp.float32)
        first = first + at * length
        return volt_ref[:, first : first + half].astype(jnp.float32)

    parts = [[], [], [], []]
    for at in span:
        halves = []
        for second in range(2):
            place = slice(second * half, (second + 1) * half)
            total = taper_ref[0:1, place] * frame(at - TAPS + 1, second)
            for tap in range(1, TAPS):
                total = total + taper_ref[tap : tap + 1, place] * frame(at + tap - TAPS + 1, second)
            halves.append(total.astype(jnp.bfloat16).astype(jnp.float32))
        for odd, value in enumerate((halves[0] + halves[1], halves[0] - halves[1])):
            main = value.astype(jnp.bfloat16).astype(jnp.float32)
            parts[2 * odd].append(main)
            parts[2 * odd + 1].append(value - main)
    for odd in range(2):
        rows = jnp.concatenate(parts[2 * odd] + parts[2 * odd + 1], axis=0)
        folded[odd] = jnp.transpose(rows).astype(jnp.bfloat16)

    part = 8
    held = part * ch_band
    shape = (2 * CORR, 2 * held)
    row = lax.broadcasted_iota(jnp.int32, shape, 0)
    column = lax.broadcasted_iota(jnp.int32, shape, 1)
    imag = column % ch_band // (ch_band // 2)
    channel = 2 * (column % (ch_band // 2)) + column // held
    band_at = column % held // ch_band
    wanted = channel - row % CORR + jnp.where(imag == row // CORR, 0, -2 * CHANNELS)

    def bands_from(at, carry):
        first = pl.multiple_of(at * group * ch_band, group * ch_band)
        products = []
        for odd in range(2):
            both = jnp.dot(
                basis_ref[odd, pl.ds(first, group * ch_band), :],
                folded[odd],
                preferred_element_type=jnp.float32,
            )
            products.append((both[:, :columns] + both[:, columns:]).astype(jnp.bfloat16))
        for begin in range(0, group, part):
            picks = [
                jnp.where(
                    (band_at == band) & (wanted == start_ref[at * group + begin + band]), 1.0, 0.0
                )
                for band in range(part)
            ]
            picked = jnp.concatenate(picks, axis=0).astype(jnp.bfloat16)
            place = slice(begin * ch_band, (begin + part) * ch_band)
            source = jnp.concatenate([p[place] for p in products], axis=0)
            spectra = jnp.dot(picked, source, preferred_element_type=jnp.float32)
            for band in range(part):
                these = spectra[band * 2 * CORR : (band + 1) * 2 * CORR].astype(jnp.bfloat16)
                if later_ref is not None:
                    later = later_ref[at * group + begin + band]
                    these = jnp.concatenate([these, later], axis=1)
                out_ref[at * group + begin + band] = these
        return carry

    lax.fori_loop(0, bands // group, bands_from, 0)


def picked_spectra(voltages, taper, basis, band_start, span, before=None, later=None):
    bands = band_start.shape[0]
    sig_dev, samples = voltages.shape
    length = taper.shape[1]
    columns = sig_dev * len(span)
    wide = columns if later is None else columns + later.shape[2]
    beside = [] if later is None else [before, later]
    whole = pl.BlockSpec(memory_space=pltpu.VMEM)
    return pl.pallas_call(
        functools.partial(spectra_kernel, 16, span),
        in_specs=[pl.BlockSpec(memory_space=pltpu.SMEM)] + [whole] * (3 + len(beside)),
        out_specs=whole,
        scratch_shapes=[pltpu.VMEM((2, length // 2, 2 * columns), jnp.bfloat16)],
        out_shape=jax.ShapeDtypeStruct((bands, 2 * CORR, wide), jnp.bfloat16),
        compiler_params=pltpu.CompilerParams(vmem_limit_bytes=VMEM_LIMIT),
        cost_estimate=pl.CostEstimate(
            flops=2 * CHANNELS * length * 2 * columns,
            bytes_accessed=2 * CHANNELS * length + 4 * sig_dev * samples,
            transcendentals=0,
        ),
    )(band_start, voltages, taper, basis, *beside)


def order_kernel(turned_ref, input_ref, out_ref, lined):
    bands, values, columns = turned_ref.shape
    signals = out_ref.shape[1]
    sig_dev = signals // bands
    frames = columns // sig_dev
    per_tile = 128 // sig_dev

    def tile(at, carry):
        lane = lax.broadcasted_iota(jnp.int32, (values, 128), 1) // sig_dev
        blocks = [turned_ref[at * per_tile + k].astype(jnp.float32) for k in range(per_tile)]
        for frame in range(frames):
            half, place = frame // per_tile, frame % per_tile
            merged = None
            for k in range(per_tile):
                piece = blocks[k][:, half * 128 : (half + 1) * 128]
                shift = (k - place) * sig_dev % 128
                if shift:
                    piece = pltpu.roll(piece, shift, 1)
                merged = piece if merged is None else jnp.where(lane == k, piece, merged)
            lined[at, frame * values : (frame + 1) * values, :] = merged
        return carry

    lax.fori_loop(0, bands // per_tile, tile, 0)
    wanted = jnp.broadcast_to(input_ref[...], (16, signals)).astype(jnp.int16)
    row = lax.broadcasted_iota(jnp.int32, (16, signals), 0).astype(jnp.int16)
    one = jnp.ones((16, signals), jnp.bfloat16)
    zero = jnp.zeros((16, signals), jnp.bfloat16)
    part = 256
    total = None
    for at in range(signals // part):
        held = jnp.concatenate([lined[2 * at], lined[2 * at + 1]], axis=1).astype(jnp.bfloat16)
        chosen = jnp.concatenate(
            [
                jnp.where(row == wanted - (at * part + first), one, zero)
                for first in range(0, part, 16)
            ],
            axis=0,
        )
        product = jnp.dot(held, chosen, preferred_element_type=jnp.float32)
        total = product if total is None else total + product
    out_ref[...] = total.astype(jnp.bfloat16)


def order_signals(turned, input_of):
    bands, values, columns = turned.shape
    signals = input_of.shape[0]
    rows = values * columns * bands // signals
    return pl.pallas_call(
        order_kernel,
        in_specs=[pl.BlockSpec(memory_space=pltpu.VMEM)] * 2,
        out_specs=pl.BlockSpec(memory_space=pltpu.VMEM),
        out_shape=jax.ShapeDtypeStruct((rows, signals), jnp.bfloat16),
        scratch_shapes=[pltpu.VMEM((signals // 128, rows, 128), jnp.float32)],
        compiler_params=pltpu.CompilerParams(vmem_limit_bytes=VMEM_LIMIT),
        cost_estimate=pl.CostEstimate(
            flops=2 * rows * signals * signals,
            bytes_accessed=4 * rows * signals,
            transcendentals=0,
        ),
    )(turned, input_of.reshape(1, signals))


def correlate_kernel(scale, count, tile, position_ref, *refs):
    blocks, before, out_ref, left = refs[:count], refs[count:-2], refs[-2], refs[-1]
    row_count = left.shape[0] // 2
    values = 2 * CORR
    step = pl.program_id(0)

    @pl.when(step == 0)
    def _():
        first = pl.multiple_of(position_ref[0] * row_count, row_count)
        own = jnp.concatenate([r[:, pl.ds(first, row_count)] for r in blocks], axis=0)
        part = 192
        row = lax.broadcasted_iota(jnp.int32, (part, part), 0)
        column = lax.broadcasted_iota(jnp.int32, (part, part), 1)
        upper = row % values < CORR
        swap = jnp.where(upper & (column == row + CORR), 1.0, 0.0)
        swap = swap - jnp.where(jnp.logical_not(upper) & (column == row - CORR), 1.0, 0.0)
        swap = swap.astype(jnp.bfloat16)
        pieces = [own[at : at + part] for at in range(0, own.shape[0], part)]
        turned = [jnp.dot(swap, p, preferred_element_type=jnp.float32) for p in pieces]
        left[:row_count] = jnp.transpose(own.astype(jnp.float32)).astype(jnp.bfloat16)
        left[row_count:] = jnp.transpose(jnp.concatenate(turned, axis=0)).astype(jnp.bfloat16)

    columns = pl.ds(pl.multiple_of(step * tile, tile), tile)
    right = jnp.concatenate([r[:, columns] for r in blocks], axis=0)
    summed = jnp.dot(left[...], right, preferred_element_type=jnp.float32)
    if before:
        summed = summed + before[0][:, columns]
    if scale is None:
        out_ref[:, columns] = summed
    else:
        summed = summed * scale
        out_ref[0, 0] = summed[:row_count].astype(jnp.bfloat16)
        out_ref[0, 1] = summed[row_count:].astype(jnp.bfloat16)


def correlate(position, blocks, row_count, before=(), scale=None):
    signals = blocks[0].shape[1]
    depth = sum(b.shape[0] for b in blocks)
    tile = 512
    whole = pl.BlockSpec(memory_space=pltpu.VMEM)
    if scale is None:
        out_spec = whole
        out_shape = jax.ShapeDtypeStruct((2 * row_count, signals), jnp.float32)
    else:
        out_spec = pl.BlockSpec((1, 2, row_count, tile), lambda g, p: (0, 0, 0, g))
        out_shape = jax.ShapeDtypeStruct((1, 2, row_count, signals), jnp.bfloat16)
    return pl.pallas_call(
        functools.partial(correlate_kernel, scale, len(blocks), tile),
        grid_spec=pltpu.PrefetchScalarGridSpec(
            num_scalar_prefetch=1,
            grid=(signals // tile,),
            in_specs=[whole] * (len(blocks) + len(before)),
            out_specs=out_spec,
            scratch_shapes=[pltpu.VMEM((2 * row_count, depth), jnp.bfloat16)],
        ),
        out_shape=out_shape,
        compiler_params=pltpu.CompilerParams(vmem_limit_bytes=VMEM_LIMIT),
        cost_estimate=pl.CostEstimate(
            flops=4 * row_count * signals * depth,
            bytes_accessed=2 * signals * depth + 8 * row_count * signals,
            transcendentals=0,
        ),
    )(position, *blocks, *before)


def from_slice(value, dx, dy):
    bands, slices = lax.axis_size("band"), lax.axis_size("tslice")
    along = slices // 2
    pairs = []
    for band in range(bands):
        way = -dx if band % 2 else dx
        for target in range(slices):
            source = ((target // 2 + way) % along) * 2 + (target % 2 + dy) % 2
            pairs.append((band * slices + source, band * slices + target))
    return lax.ppermute(value, ("band", "tslice"), pairs)


def gather_and_correlate(own, position, row_count, scale):
    take = from_slice
    near = (take(own, 1, 0), take(own, 0, 1), take(own, -1, 0))
    right, other, left = near
    summed = correlate(position, [own, right, other, left], row_count)
    right_other, left_other, far = take(right, 0, 1), take(other, -1, 0), take(right, 1, 0)
    left_other, summed = lax.optimization_barrier((left_other, summed))
    cut = own.shape[0] * 2 // 3
    last = [take(left_other[:cut], -1, 0), take(right_other[cut:], 1, 0)]
    summed = correlate(position, [right_other, left_other, far], row_count, [summed])
    return correlate(position, last, row_count, [summed], scale)


def on_device(voltages, taper, input_of, band_start):
    length = 2 * CHANNELS
    bands = lax.axis_size("band")
    slices = lax.axis_size("tslice")
    frames = voltages.shape[1] // length
    signals = input_of.shape[0]
    position = lax.axis_index("tslice")
    tail = voltages[:, (frames - TAPS + 1) * length :]
    before = lax.ppermute(tail, "tslice", [(s, s + 1) for s in range(slices - 1)])
    basis = jnp.asarray(make_basis(bands, length))
    half = frames // 2
    transform = functools.partial(picked_spectra, voltages, taper, basis, band_start)
    later = transform(tuple(range(half, frames)))
    spectra = transform(tuple(range(half)), before, later)
    turned = lax.all_to_all(spectra, "band", split_axis=0, concat_axis=0, tiled=True)
    own = order_signals(turned, input_of)
    position = position.astype(jnp.int32).reshape(1)
    scale = 1.0 / (CORR * frames * slices)
    return gather_and_correlate(own, position, signals // slices, scale)


def solution(mesh):
    return jax.shard_map(
        on_device,
        mesh=mesh,
        in_specs=(P("band", "tslice"), P(), P(), P()),
        out_specs=P("band", None, "tslice", None),
        check_vma=False,
    )
```

```python
import functools

import jax
import jax.numpy as jnp
import numpy as np
from jax import lax
from jax.experimental import pallas as pl
from jax.experimental.pallas import tpu as pltpu
from jax.sharding import PartitionSpec as P

CHANNELS = 1024
TAPS = 4
CORR = 12
VMEM_LIMIT = 16 << 20


def make_basis(bands, length):
    half = length // 2
    index = np.arange(half, dtype=np.int64)
    m = (np.arange(CHANNELS, dtype=np.int64)[:, None] * index[None, :]) % length
    phases = np.float32(2.0 * np.pi / length) * m.astype(np.float32)
    stacked = np.stack([np.cos(phases), -np.sin(phases)], axis=0)
    stacked = stacked.reshape(2, bands, CHANNELS // bands // 2, 2, half)
    stacked = stacked.transpose(3, 1, 0, 2, 4).reshape(2, CHANNELS, half)
    return stacked.astype(jnp.bfloat16)


def spectra_kernel(group, span, start_ref, volt_ref, taper_ref, basis_ref, *refs):
    out_ref, folded = refs[-2:]
    before_ref, later_ref = refs[:2] if len(refs) == 4 else (None, None)
    sig_dev = volt_ref.shape[0]
    length = taper_ref.shape[1]
    half = length // 2
    bands = out_ref.shape[0]
    columns = sig_dev * len(span)
    ch_band = basis_ref.shape[1] // bands

    def frame(at, second):
        first = second * half
        if at < 0:
            first = first + (at + TAPS - 1) * length
            return before_ref[:, first : first + half].astype(jnp.float32)
        first = first + at * length
        return volt_ref[:, first : first + half].astype(jnp.float32)

    parts = [[], [], [], []]
    for at in span:
        halves = []
        for second in range(2):
            place = slice(second * half, (second + 1) * half)
            total = taper_ref[0:1, place] * frame(at - TAPS + 1, second)
            for tap in range(1, TAPS):
                total = total + taper_ref[tap : tap + 1, place] * frame(at + tap - TAPS + 1, second)
            halves.append(total.astype(jnp.bfloat16).astype(jnp.float32))
        for odd, value in enumerate((halves[0] + halves[1], halves[0] - halves[1])):
            main = value.astype(jnp.bfloat16)
            parts[2 * odd].append(main)
            parts[2 * odd + 1].append((value - main.astype(jnp.float32)).astype(jnp.bfloat16))
    for odd in range(2):
        rows = jnp.concatenate(parts[2 * odd] + parts[2 * odd + 1], axis=0)
        folded[odd] = jnp.transpose(rows)

    part = 8
    held = part * ch_band
    shape = (2 * CORR, 2 * held)
    row = lax.broadcasted_iota(jnp.int32, shape, 0)
    column = lax.broadcasted_iota(jnp.int32, shape, 1)
    imag = column % ch_band // (ch_band // 2)
    channel = 2 * (column % (ch_band // 2)) + column // held
    band_at = column % held // ch_band
    wanted = channel - row % CORR + jnp.where(imag == row // CORR, 0, -2 * CHANNELS)

    def bands_from(at, carry):
        first = pl.multiple_of(at * group * ch_band, group * ch_band)
        products = []
        for odd in range(2):
            both = jnp.dot(
                basis_ref[odd, pl.ds(first, group * ch_band), :],
                folded[odd],
                preferred_element_type=jnp.float32,
            )
            products.append((both[:, :columns] + both[:, columns:]).astype(jnp.bfloat16))
        for begin in range(0, group, part):
            picks = [
                jnp.where(
                    (band_at == band) & (wanted == start_ref[at * group + begin + band]), 1.0, 0.0
                )
                for band in range(part)
            ]
            picked = jnp.concatenate(picks, axis=0).astype(jnp.bfloat16)
            place = slice(begin * ch_band, (begin + part) * ch_band)
            source = jnp.concatenate([p[place] for p in products], axis=0)
            spectra = jnp.dot(picked, source, preferred_element_type=jnp.float32)
            for band in range(part):
                these = spectra[band * 2 * CORR : (band + 1) * 2 * CORR].astype(jnp.bfloat16)
                if later_ref is not None:
                    later = later_ref[at * group + begin + band]
                    these = jnp.concatenate([these, later], axis=1)
                out_ref[at * group + begin + band] = these
        return carry

    lax.fori_loop(0, bands // group, bands_from, 0)


def picked_spectra(voltages, taper, basis, band_start, span, before=None, later=None):
    bands = band_start.shape[0]
    sig_dev, samples = voltages.shape
    length = taper.shape[1]
    columns = sig_dev * len(span)
    wide = columns if later is None else columns + later.shape[2]
    beside = [] if later is None else [before, later]
    whole = pl.BlockSpec(memory_space=pltpu.VMEM)
    return pl.pallas_call(
        functools.partial(spectra_kernel, 16, span),
        in_specs=[pl.BlockSpec(memory_space=pltpu.SMEM)] + [whole] * (3 + len(beside)),
        out_specs=whole,
        scratch_shapes=[pltpu.VMEM((2, length // 2, 2 * columns), jnp.bfloat16)],
        out_shape=jax.ShapeDtypeStruct((bands, 2 * CORR, wide), jnp.bfloat16),
        compiler_params=pltpu.CompilerParams(vmem_limit_bytes=VMEM_LIMIT),
        cost_estimate=pl.CostEstimate(
            flops=2 * CHANNELS * length * 2 * columns,
            bytes_accessed=2 * CHANNELS * length + 4 * sig_dev * samples,
            transcendentals=0,
        ),
    )(band_start, voltages, taper, basis, *beside)


def order_kernel(turned_ref, input_ref, out_ref, lined):
    bands, values, columns = turned_ref.shape
    signals = out_ref.shape[1]
    sig_dev = signals // bands
    frames = columns // sig_dev
    per_tile = 128 // sig_dev

    def tile(at, carry):
        lane = lax.broadcasted_iota(jnp.int32, (values, 128), 1) // sig_dev
        blocks = [turned_ref[at * per_tile + k].astype(jnp.float32) for k in range(per_tile)]
        for frame in range(frames):
            half, place = frame // per_tile, frame % per_tile
            merged = None
            for k in range(per_tile):
                piece = blocks[k][:, half * 128 : (half + 1) * 128]
                shift = (k - place) * sig_dev % 128
                if shift:
                    piece = pltpu.roll(piece, shift, 1)
                merged = piece if merged is None else jnp.where(lane == k, piece, merged)
            lined[at, frame * values : (frame + 1) * values, :] = merged
        return carry

    lax.fori_loop(0, bands // per_tile, tile, 0)
    held = jnp.concatenate([lined[at].astype(jnp.bfloat16) for at in range(signals // 128)], axis=1)
    part = 512
    row = lax.broadcasted_iota(jnp.int32, (16, part), 0).astype(jnp.int16)
    one = jnp.ones((16, part), jnp.bfloat16)
    zero = jnp.zeros((16, part), jnp.bfloat16)
    for at in range(0, signals, part):
        wanted = jnp.broadcast_to(input_ref[:, at : at + part], (16, part)).astype(jnp.int16)
        chosen = jnp.concatenate(
            [jnp.where(row == wanted - first, one, zero) for first in range(0, signals, 16)], axis=0
        )
        out_ref[:, at : at + part] = jnp.dot(
            held, chosen, preferred_element_type=jnp.float32
        ).astype(jnp.bfloat16)


def order_signals(turned, input_of):
    bands, values, columns = turned.shape
    signals = input_of.shape[0]
    rows = values * columns * bands // signals
    return pl.pallas_call(
        order_kernel,
        in_specs=[pl.BlockSpec(memory_space=pltpu.VMEM)] * 2,
        out_specs=pl.BlockSpec(memory_space=pltpu.VMEM),
        out_shape=jax.ShapeDtypeStruct((rows, signals), jnp.bfloat16),
        scratch_shapes=[pltpu.VMEM((signals // 128, rows, 128), jnp.float32)],
        compiler_params=pltpu.CompilerParams(vmem_limit_bytes=VMEM_LIMIT),
        cost_estimate=pl.CostEstimate(
            flops=2 * rows * signals * signals,
            bytes_accessed=4 * rows * signals,
            transcendentals=0,
        ),
    )(turned, input_of.reshape(1, signals))


def correlate_kernel(scale, count, tile, position_ref, *refs):
    blocks, before, out_ref, left = refs[:count], refs[count:-2], refs[-2], refs[-1]
    row_count = left.shape[0] // 2
    values = 2 * CORR
    step = pl.program_id(0)

    @pl.when(step == 0)
    def _():
        first = pl.multiple_of(position_ref[0] * row_count, row_count)
        own = jnp.concatenate([r[:, pl.ds(first, row_count)] for r in blocks], axis=0)
        part = 192
        row = lax.broadcasted_iota(jnp.int32, (part, part), 0)
        column = lax.broadcasted_iota(jnp.int32, (part, part), 1)
        upper = row % values < CORR
        swap = jnp.where(upper & (column == row + CORR), 1.0, 0.0)
        swap = swap - jnp.where(jnp.logical_not(upper) & (column == row - CORR), 1.0, 0.0)
        swap = swap.astype(jnp.bfloat16)
        pieces = [own[at : at + part] for at in range(0, own.shape[0], part)]
        turned = [jnp.dot(swap, p, preferred_element_type=jnp.float32) for p in pieces]
        left[:row_count] = jnp.transpose(own.astype(jnp.float32)).astype(jnp.bfloat16)
        left[row_count:] = jnp.transpose(jnp.concatenate(turned, axis=0)).astype(jnp.bfloat16)

    columns = pl.ds(pl.multiple_of(step * tile, tile), tile)
    right = jnp.concatenate([r[:, columns] for r in blocks], axis=0)
    summed = jnp.dot(left[...], right, preferred_element_type=jnp.float32)
    if before:
        summed = summed + before[0][:, columns]
    if scale is None:
        out_ref[:, columns] = summed
    else:
        summed = summed * scale
        out_ref[0, 0] = summed[:row_count].astype(jnp.bfloat16)
        out_ref[0, 1] = summed[row_count:].astype(jnp.bfloat16)


def correlate(position, blocks, row_count, before=(), scale=None):
    signals = blocks[0].shape[1]
    depth = sum(b.shape[0] for b in blocks)
    tile = 512 if scale is None else 1024
    whole = pl.BlockSpec(memory_space=pltpu.VMEM)
    if scale is None:
        out_spec = whole
        out_shape = jax.ShapeDtypeStruct((2 * row_count, signals), jnp.float32)
    else:
        out_spec = pl.BlockSpec((1, 2, row_count, tile), lambda g, p: (0, 0, 0, g))
        out_shape = jax.ShapeDtypeStruct((1, 2, row_count, signals), jnp.bfloat16)
    return pl.pallas_call(
        functools.partial(correlate_kernel, scale, len(blocks), tile),
        grid_spec=pltpu.PrefetchScalarGridSpec(
            num_scalar_prefetch=1,
            grid=(signals // tile,),
            in_specs=[whole] * (len(blocks) + len(before)),
            out_specs=out_spec,
            scratch_shapes=[pltpu.VMEM((2 * row_count, depth), jnp.bfloat16)],
        ),
        out_shape=out_shape,
        compiler_params=pltpu.CompilerParams(vmem_limit_bytes=VMEM_LIMIT),
        cost_estimate=pl.CostEstimate(
            flops=4 * row_count * signals * depth,
            bytes_accessed=2 * signals * depth + 8 * row_count * signals,
            transcendentals=0,
        ),
    )(position, *blocks, *before)


def from_slice(value, dx, dy):
    bands, slices = lax.axis_size("band"), lax.axis_size("tslice")
    along = slices // 2
    pairs = []
    for band in range(bands):
        way = -dx if band % 2 else dx
        for target in range(slices):
            source = ((target // 2 + way) % along) * 2 + (target % 2 + dy) % 2
            pairs.append((band * slices + source, band * slices + target))
    return lax.ppermute(value, ("band", "tslice"), pairs)


def gather_and_correlate(own, position, row_count, scale):
    take = from_slice
    near = (take(own, 1, 0), take(own, 0, 1), take(own, -1, 0))
    right, other, left = near
    summed = correlate(position, [own, right, other, left], row_count)
    right_other, left_other, far = take(right, 0, 1), take(other, -1, 0), take(right, 1, 0)
    right_other, summed = lax.optimization_barrier((right_other, summed))
    cut = own.shape[0] * 2 // 3
    last = [take(right_other[:cut], 1, 0), take(far[cut:], 0, 1)]
    summed = correlate(position, [right_other, left_other, far], row_count, [summed])
    return correlate(position, last, row_count, [summed], scale)


def on_device(voltages, taper, input_of, band_start):
    length = 2 * CHANNELS
    bands = lax.axis_size("band")
    slices = lax.axis_size("tslice")
    frames = voltages.shape[1] // length
    signals = input_of.shape[0]
    position = lax.axis_index("tslice")
    tail = voltages[:, (frames - TAPS + 1) * length :]
    before = lax.ppermute(tail, "tslice", [(s, s + 1) for s in range(slices - 1)])
    basis = jnp.asarray(make_basis(bands, length))
    half = frames // 2
    transform = functools.partial(picked_spectra, voltages, taper, basis, band_start)
    later = transform(tuple(range(half, frames)))
    spectra = transform(tuple(range(half)), before, later)
    turned = lax.all_to_all(spectra, "band", split_axis=0, concat_axis=0, tiled=True)
    own = order_signals(turned, input_of)
    position = position.astype(jnp.int32).reshape(1)
    scale = 1.0 / (CORR * frames * slices)
    return gather_and_correlate(own, position, signals // slices, scale)


def solution(mesh):
    return jax.shard_map(
        on_device,
        mesh=mesh,
        in_specs=(P("band", "tslice"), P(), P(), P()),
        out_specs=P("band", None, "tslice", None),
        check_vma=False,
    )
```

```python
import functools

import jax
import jax.numpy as jnp
import numpy as np
from jax import lax
from jax.experimental import pallas as pl
from jax.experimental.pallas import tpu as pltpu
from jax.sharding import PartitionSpec as P

CHANNELS = 1024
TAPS = 4
CORR = 12
VMEM_LIMIT = 16 << 20


def make_basis(bands, length):
    half = length // 2
    index = np.arange(half, dtype=np.int64)
    m = (np.arange(CHANNELS, dtype=np.int64)[:, None] * index[None, :]) % length
    phases = np.float32(2.0 * np.pi / length) * m.astype(np.float32)
    stacked = np.stack([np.cos(phases), -np.sin(phases)], axis=0)
    stacked = stacked.reshape(2, bands, CHANNELS // bands // 2, 2, half)
    stacked = stacked.transpose(3, 1, 0, 2, 4).reshape(2, CHANNELS, half)
    return stacked.astype(jnp.bfloat16)


def spectra_kernel(group, span, start_ref, volt_ref, taper_ref, basis_ref, *refs):
    out_ref, folded = refs[-2:]
    before_ref, later_ref = refs[:2] if len(refs) == 4 else (None, None)
    sig_dev = volt_ref.shape[0]
    length = taper_ref.shape[1]
    half = length // 2
    bands = out_ref.shape[0]
    columns = sig_dev * len(span)
    ch_band = basis_ref.shape[1] // bands

    def frame(at, second):
        first = second * half
        if at < 0:
            first = first + (at + TAPS - 1) * length
            return before_ref[:, first : first + half].astype(jnp.float32)
        first = first + at * length
        return volt_ref[:, first : first + half].astype(jnp.float32)

    parts = [[], [], [], []]
    for at in span:
        halves = []
        for second in range(2):
            place = slice(second * half, (second + 1) * half)
            total = taper_ref[0:1, place] * frame(at - TAPS + 1, second)
            for tap in range(1, TAPS):
                total = total + taper_ref[tap : tap + 1, place] * frame(at + tap - TAPS + 1, second)
            halves.append(total.astype(jnp.bfloat16).astype(jnp.float32))
        for odd, value in enumerate((halves[0] + halves[1], halves[0] - halves[1])):
            main = value.astype(jnp.bfloat16)
            parts[2 * odd].append(main)
            parts[2 * odd + 1].append((value - main.astype(jnp.float32)).astype(jnp.bfloat16))
    for odd in range(2):
        rows = jnp.concatenate(parts[2 * odd] + parts[2 * odd + 1], axis=0)
        folded[odd] = jnp.transpose(rows)

    part = 8
    held = part * ch_band
    shape = (2 * CORR, 2 * held)
    row = lax.broadcasted_iota(jnp.int32, shape, 0)
    column = lax.broadcasted_iota(jnp.int32, shape, 1)
    imag = column % ch_band // (ch_band // 2)
    channel = 2 * (column % (ch_band // 2)) + column // held
    band_at = column % held // ch_band
    wanted = channel - row % CORR + jnp.where(imag == row // CORR, 0, -2 * CHANNELS)

    def bands_from(at, carry):
        first = pl.multiple_of(at * group * ch_band, group * ch_band)
        products = []
        for odd in range(2):
            both = jnp.dot(
                basis_ref[odd, pl.ds(first, group * ch_band), :],
                folded[odd],
                preferred_element_type=jnp.float32,
            )
            products.append((both[:, :columns] + both[:, columns:]).astype(jnp.bfloat16))
        for begin in range(0, group, part):
            picks = [
                jnp.where(
                    (band_at == band) & (wanted == start_ref[at * group + begin + band]), 1.0, 0.0
                )
                for band in range(part)
            ]
            picked = jnp.concatenate(picks, axis=0).astype(jnp.bfloat16)
            place = slice(begin * ch_band, (begin + part) * ch_band)
            source = jnp.concatenate([p[place] for p in products], axis=0)
            spectra = jnp.dot(picked, source, preferred_element_type=jnp.float32)
            for band in range(part):
                these = spectra[band * 2 * CORR : (band + 1) * 2 * CORR].astype(jnp.bfloat16)
                if later_ref is not None:
                    later = later_ref[at * group + begin + band]
                    these = jnp.concatenate([these, later], axis=1)
                out_ref[at * group + begin + band] = these
        return carry

    lax.fori_loop(0, bands // group, bands_from, 0, unroll=True)


def picked_spectra(voltages, taper, basis, band_start, span, before=None, later=None):
    bands = band_start.shape[0]
    sig_dev, samples = voltages.shape
    length = taper.shape[1]
    columns = sig_dev * len(span)
    wide = columns if later is None else columns + later.shape[2]
    beside = [] if later is None else [before, later]
    whole = pl.BlockSpec(memory_space=pltpu.VMEM)
    return pl.pallas_call(
        functools.partial(spectra_kernel, 16, span),
        in_specs=[pl.BlockSpec(memory_space=pltpu.SMEM)] + [whole] * (3 + len(beside)),
        out_specs=whole,
        scratch_shapes=[pltpu.VMEM((2, length // 2, 2 * columns), jnp.bfloat16)],
        out_shape=jax.ShapeDtypeStruct((bands, 2 * CORR, wide), jnp.bfloat16),
        compiler_params=pltpu.CompilerParams(vmem_limit_bytes=VMEM_LIMIT),
        cost_estimate=pl.CostEstimate(
            flops=2 * CHANNELS * length * 2 * columns,
            bytes_accessed=2 * CHANNELS * length + 4 * sig_dev * samples,
            transcendentals=0,
        ),
    )(band_start, voltages, taper, basis, *beside)


def order_kernel(turned_ref, input_ref, out_ref, lined):
    bands, values, columns = turned_ref.shape
    signals = out_ref.shape[1]
    sig_dev = signals // bands
    frames = columns // sig_dev
    per_tile = 128 // sig_dev

    def tile(at, carry):
        lane = lax.broadcasted_iota(jnp.int32, (values, 128), 1) // sig_dev
        blocks = [turned_ref[at * per_tile + k].astype(jnp.float32) for k in range(per_tile)]
        for frame in range(frames):
            half, place = frame // per_tile, frame % per_tile
            merged = None
            for k in range(per_tile):
                piece = blocks[k][:, half * 128 : (half + 1) * 128]
                shift = (k - place) * sig_dev % 128
                if shift:
                    piece = pltpu.roll(piece, shift, 1)
                merged = piece if merged is None else jnp.where(lane == k, piece, merged)
            lined[at, frame * values : (frame + 1) * values, :] = merged
        return carry

    lax.fori_loop(0, bands // per_tile, tile, 0, unroll=True)
    held = jnp.concatenate([lined[at].astype(jnp.bfloat16) for at in range(signals // 128)], axis=1)
    part = 512
    row = lax.broadcasted_iota(jnp.int32, (16, part), 0).astype(jnp.int16)
    one = jnp.ones((16, part), jnp.bfloat16)
    zero = jnp.zeros((16, part), jnp.bfloat16)
    for at in range(0, signals, part):
        wanted = jnp.broadcast_to(input_ref[:, at : at + part], (16, part)).astype(jnp.int16)
        chosen = jnp.concatenate(
            [jnp.where(row == wanted - first, one, zero) for first in range(0, signals, 16)], axis=0
        )
        out_ref[:, at : at + part] = jnp.dot(
            held, chosen, preferred_element_type=jnp.float32
        ).astype(jnp.bfloat16)


def order_signals(turned, input_of):
    bands, values, columns = turned.shape
    signals = input_of.shape[0]
    rows = values * columns * bands // signals
    return pl.pallas_call(
        order_kernel,
        in_specs=[pl.BlockSpec(memory_space=pltpu.VMEM)] * 2,
        out_specs=pl.BlockSpec(memory_space=pltpu.VMEM),
        out_shape=jax.ShapeDtypeStruct((rows, signals), jnp.bfloat16),
        scratch_shapes=[pltpu.VMEM((signals // 128, rows, 128), jnp.float32)],
        compiler_params=pltpu.CompilerParams(vmem_limit_bytes=VMEM_LIMIT),
        cost_estimate=pl.CostEstimate(
            flops=2 * rows * signals * signals,
            bytes_accessed=4 * rows * signals,
            transcendentals=0,
        ),
    )(turned, input_of.reshape(1, signals))


def correlate_kernel(scale, count, tile, position_ref, *refs):
    blocks, before, out_ref, left = refs[:count], refs[count:-2], refs[-2], refs[-1]
    row_count = left.shape[0] // 2
    values = 2 * CORR
    step = pl.program_id(0)

    @pl.when(step == 0)
    def _():
        first = pl.multiple_of(position_ref[0] * row_count, row_count)
        own = jnp.concatenate([r[:, pl.ds(first, row_count)] for r in blocks], axis=0)
        part = 192
        row = lax.broadcasted_iota(jnp.int32, (part, part), 0)
        column = lax.broadcasted_iota(jnp.int32, (part, part), 1)
        upper = row % values < CORR
        swap = jnp.where(upper & (column == row + CORR), 1.0, 0.0)
        swap = swap - jnp.where(jnp.logical_not(upper) & (column == row - CORR), 1.0, 0.0)
        swap = swap.astype(jnp.bfloat16)
        pieces = [own[at : at + part] for at in range(0, own.shape[0], part)]
        turned = [jnp.dot(swap, p, preferred_element_type=jnp.float32) for p in pieces]
        left[:row_count] = jnp.transpose(own.astype(jnp.float32)).astype(jnp.bfloat16)
        left[row_count:] = jnp.transpose(jnp.concatenate(turned, axis=0)).astype(jnp.bfloat16)

    columns = pl.ds(pl.multiple_of(step * tile, tile), tile)
    right = jnp.concatenate([r[:, columns] for r in blocks], axis=0)
    summed = jnp.dot(left[...], right, preferred_element_type=jnp.float32)
    if before:
        summed = summed + before[0][:, columns]
    if scale is None:
        out_ref[:, columns] = summed
    else:
        summed = summed * scale
        out_ref[0, 0] = summed[:row_count].astype(jnp.bfloat16)
        out_ref[0, 1] = summed[row_count:].astype(jnp.bfloat16)


def correlate(position, blocks, row_count, before=(), scale=None):
    signals = blocks[0].shape[1]
    depth = sum(b.shape[0] for b in blocks)
    tile = 1024
    whole = pl.BlockSpec(memory_space=pltpu.VMEM)
    if scale is None:
        out_spec = whole
        out_shape = jax.ShapeDtypeStruct((2 * row_count, signals), jnp.float32)
    else:
        out_spec = pl.BlockSpec((1, 2, row_count, tile), lambda g, p: (0, 0, 0, g))
        out_shape = jax.ShapeDtypeStruct((1, 2, row_count, signals), jnp.bfloat16)
    return pl.pallas_call(
        functools.partial(correlate_kernel, scale, len(blocks), tile),
        grid_spec=pltpu.PrefetchScalarGridSpec(
            num_scalar_prefetch=1,
            grid=(signals // tile,),
            in_specs=[whole] * (len(blocks) + len(before)),
            out_specs=out_spec,
            scratch_shapes=[pltpu.VMEM((2 * row_count, depth), jnp.bfloat16)],
        ),
        out_shape=out_shape,
        compiler_params=pltpu.CompilerParams(vmem_limit_bytes=VMEM_LIMIT),
        cost_estimate=pl.CostEstimate(
            flops=4 * row_count * signals * depth,
            bytes_accessed=2 * signals * depth + 8 * row_count * signals,
            transcendentals=0,
        ),
    )(position, *blocks, *before)


def from_slice(value, dx, dy):
    bands, slices = lax.axis_size("band"), lax.axis_size("tslice")
    along = slices // 2
    pairs = []
    for band in range(bands):
        way = -dx if band % 2 else dx
        for target in range(slices):
            source = ((target // 2 + way) % along) * 2 + (target % 2 + dy) % 2
            pairs.append((band * slices + source, band * slices + target))
    return lax.ppermute(value, ("band", "tslice"), pairs)


def gather_and_correlate(own, position, row_count, scale):
    take = from_slice
    near = (take(own, 1, 0), take(own, 0, 1), take(own, -1, 0))
    right, other, left = near
    summed = correlate(position, [own], row_count)
    summed = correlate(position, [right, other, left], row_count, [summed])
    right_other, left_other, far = take(right, 0, 1), take(other, -1, 0), take(right, 1, 0)
    right_other, summed = lax.optimization_barrier((right_other, summed))
    cut = own.shape[0] * 3 // 4
    last = [take(right_other[:cut], 1, 0), take(far[cut:], 0, 1)]
    summed = correlate(position, [right_other, left_other, far], row_count, [summed])
    return correlate(position, last, row_count, [summed], scale)


def on_device(voltages, taper, input_of, band_start):
    length = 2 * CHANNELS
    bands = lax.axis_size("band")
    slices = lax.axis_size("tslice")
    frames = voltages.shape[1] // length
    signals = input_of.shape[0]
    position = lax.axis_index("tslice")
    tail = voltages[:, (frames - TAPS + 1) * length :]
    before = lax.ppermute(tail, "tslice", [(s, s + 1) for s in range(slices - 1)])
    basis = jnp.asarray(make_basis(bands, length))
    half = frames // 2
    transform = functools.partial(picked_spectra, voltages, taper, basis, band_start)
    later = transform(tuple(range(half, frames)))
    spectra = transform(tuple(range(half)), before, later)
    turned = lax.all_to_all(spectra, "band", split_axis=0, concat_axis=0, tiled=True)
    own = order_signals(turned, input_of)
    position = position.astype(jnp.int32).reshape(1)
    scale = 1.0 / (CORR * frames * slices)
    return gather_and_correlate(own, position, signals // slices, scale)


def solution(mesh):
    return jax.shard_map(
        on_device,
        mesh=mesh,
        in_specs=(P("band", "tslice"), P(), P(), P()),
        out_specs=P("band", None, "tslice", None),
        check_vma=False,
    )
```

```python
import functools

import jax
import jax.numpy as jnp
import numpy as np
from jax import lax
from jax.experimental import pallas as pl
from jax.experimental.pallas import tpu as pltpu
from jax.sharding import PartitionSpec as P

CHANNELS = 1024
TAPS = 4
CORR = 12
VMEM_LIMIT = 16 << 20


def make_basis(bands, length):
    half = length // 2
    index = np.arange(half, dtype=np.int64)
    m = (np.arange(CHANNELS, dtype=np.int64)[:, None] * index[None, :]) % length
    phases = np.float32(2.0 * np.pi / length) * m.astype(np.float32)
    stacked = np.stack([np.cos(phases), -np.sin(phases)], axis=0)
    stacked = stacked.reshape(2, bands, CHANNELS // bands // 2, 2, half)
    stacked = stacked.transpose(3, 1, 0, 2, 4).reshape(2, CHANNELS, half)
    return stacked.astype(jnp.bfloat16)


def spectra_kernel(group, span, start_ref, volt_ref, taper_ref, basis_ref, *refs):
    out_ref, folded = refs[-2:]
    before_ref, later_ref = refs[:2] if len(refs) == 4 else (None, None)
    sig_dev = volt_ref.shape[0]
    length = taper_ref.shape[1]
    half = length // 2
    bands = out_ref.shape[0]
    columns = sig_dev * len(span)
    ch_band = basis_ref.shape[1] // bands

    def frame(at, second):
        first = second * half
        if at < 0:
            first = first + (at + TAPS - 1) * length
            return before_ref[:, first : first + half].astype(jnp.float32)
        first = first + at * length
        return volt_ref[:, first : first + half].astype(jnp.float32)

    parts = [[], [], [], []]
    for at in span:
        halves = []
        for second in range(2):
            place = slice(second * half, (second + 1) * half)
            total = taper_ref[0:1, place] * frame(at - TAPS + 1, second)
            for tap in range(1, TAPS):
                total = total + taper_ref[tap : tap + 1, place] * frame(at + tap - TAPS + 1, second)
            halves.append(total.astype(jnp.bfloat16).astype(jnp.float32))
        for odd, value in enumerate((halves[0] + halves[1], halves[0] - halves[1])):
            main = value.astype(jnp.bfloat16)
            parts[2 * odd].append(main)
            parts[2 * odd + 1].append((value - main.astype(jnp.float32)).astype(jnp.bfloat16))
    for odd in range(2):
        rows = jnp.concatenate(parts[2 * odd] + parts[2 * odd + 1], axis=0)
        folded[odd] = jnp.transpose(rows)

    part = 8
    held = part * ch_band
    shape = (2 * CORR, 2 * held)
    row = lax.broadcasted_iota(jnp.int32, shape, 0)
    column = lax.broadcasted_iota(jnp.int32, shape, 1)
    imag = column % ch_band // (ch_band // 2)
    channel = 2 * (column % (ch_band // 2)) + column // held
    band_at = column % held // ch_band
    wanted = channel - row % CORR + jnp.where(imag == row // CORR, 0, -2 * CHANNELS)

    def bands_from(at, carry):
        first = pl.multiple_of(at * group * ch_band, group * ch_band)
        products = []
        for odd in range(2):
            both = jnp.dot(
                basis_ref[odd, pl.ds(first, group * ch_band), :],
                folded[odd],
                preferred_element_type=jnp.float32,
            )
            products.append((both[:, :columns] + both[:, columns:]).astype(jnp.bfloat16))
        for begin in range(0, group, part):
            picks = [
                jnp.where(
                    (band_at == band) & (wanted == start_ref[at * group + begin + band]), 1.0, 0.0
                )
                for band in range(part)
            ]
            picked = jnp.concatenate(picks, axis=0).astype(jnp.bfloat16)
            place = slice(begin * ch_band, (begin + part) * ch_band)
            source = jnp.concatenate([p[place] for p in products], axis=0)
            spectra = jnp.dot(picked, source, preferred_element_type=jnp.float32)
            for band in range(part):
                these = spectra[band * 2 * CORR : (band + 1) * 2 * CORR].astype(jnp.bfloat16)
                if later_ref is not None:
                    later = later_ref[at * group + begin + band]
                    these = jnp.concatenate([these, later], axis=1)
                out_ref[at * group + begin + band] = these
        return carry

    lax.fori_loop(0, bands // group, bands_from, 0, unroll=True)


def picked_spectra(voltages, taper, basis, band_start, span, before=None, later=None):
    bands = band_start.shape[0]
    sig_dev, samples = voltages.shape
    length = taper.shape[1]
    columns = sig_dev * len(span)
    wide = columns if later is None else columns + later.shape[2]
    beside = [] if later is None else [before, later]
    whole = pl.BlockSpec(memory_space=pltpu.VMEM)
    return pl.pallas_call(
        functools.partial(spectra_kernel, 16, span),
        in_specs=[pl.BlockSpec(memory_space=pltpu.SMEM)] + [whole] * (3 + len(beside)),
        out_specs=whole,
        scratch_shapes=[pltpu.VMEM((2, length // 2, 2 * columns), jnp.bfloat16)],
        out_shape=jax.ShapeDtypeStruct((bands, 2 * CORR, wide), jnp.bfloat16),
        compiler_params=pltpu.CompilerParams(vmem_limit_bytes=VMEM_LIMIT),
        cost_estimate=pl.CostEstimate(
            flops=2 * CHANNELS * length * 2 * columns,
            bytes_accessed=2 * CHANNELS * length + 4 * sig_dev * samples,
            transcendentals=0,
        ),
    )(band_start, voltages, taper, basis, *beside)


def order_kernel(turned_ref, input_ref, out_ref, lined):
    bands, values, columns = turned_ref.shape
    signals = out_ref.shape[1]
    sig_dev = signals // bands
    frames = columns // sig_dev
    per_tile = 128 // sig_dev

    def tile(at, carry):
        lane = lax.broadcasted_iota(jnp.int32, (values, 128), 1) // sig_dev
        blocks = [turned_ref[at * per_tile + k].astype(jnp.float32) for k in range(per_tile)]
        for frame in range(frames):
            half, place = frame // per_tile, frame % per_tile
            merged = None
            for k in range(per_tile):
                piece = blocks[k][:, half * 128 : (half + 1) * 128]
                shift = (k - place) * sig_dev % 128
                if shift:
                    piece = pltpu.roll(piece, shift, 1)
                merged = piece if merged is None else jnp.where(lane == k, piece, merged)
            lined[at, frame * values : (frame + 1) * values, :] = merged
        return carry

    lax.fori_loop(0, bands // per_tile, tile, 0, unroll=True)
    held = jnp.concatenate([lined[at].astype(jnp.bfloat16) for at in range(signals // 128)], axis=1)
    part = 512
    row = lax.broadcasted_iota(jnp.int32, (16, part), 0).astype(jnp.int16)
    one = jnp.ones((16, part), jnp.bfloat16)
    zero = jnp.zeros((16, part), jnp.bfloat16)
    for at in range(0, signals, part):
        wanted = jnp.broadcast_to(input_ref[:, at : at + part], (16, part)).astype(jnp.int16)
        chosen = jnp.concatenate(
            [jnp.where(row == wanted - first, one, zero) for first in range(0, signals, 16)], axis=0
        )
        out_ref[:, at : at + part] = jnp.dot(
            held, chosen, preferred_element_type=jnp.float32
        ).astype(jnp.bfloat16)


def order_signals(turned, input_of):
    bands, values, columns = turned.shape
    signals = input_of.shape[0]
    rows = values * columns * bands // signals
    return pl.pallas_call(
        order_kernel,
        in_specs=[pl.BlockSpec(memory_space=pltpu.VMEM)] * 2,
        out_specs=pl.BlockSpec(memory_space=pltpu.VMEM),
        out_shape=jax.ShapeDtypeStruct((rows, signals), jnp.bfloat16),
        scratch_shapes=[pltpu.VMEM((signals // 128, rows, 128), jnp.float32)],
        compiler_params=pltpu.CompilerParams(vmem_limit_bytes=VMEM_LIMIT),
        cost_estimate=pl.CostEstimate(
            flops=2 * rows * signals * signals,
            bytes_accessed=4 * rows * signals,
            transcendentals=0,
        ),
    )(turned, input_of.reshape(1, signals))


def correlate_kernel(scale, count, tile, position_ref, *refs):
    blocks, before, out_ref, left = refs[:count], refs[count:-2], refs[-2], refs[-1]
    row_count = left.shape[0] // 2
    values = 2 * CORR
    step = pl.program_id(0)

    @pl.when(step == 0)
    def _():
        first = pl.multiple_of(position_ref[0] * row_count, row_count)
        own = jnp.concatenate([r[:, pl.ds(first, row_count)] for r in blocks], axis=0)
        part = 192
        row = lax.broadcasted_iota(jnp.int32, (part, part), 0)
        column = lax.broadcasted_iota(jnp.int32, (part, part), 1)
        upper = row % values < CORR
        swap = jnp.where(upper & (column == row + CORR), 1.0, 0.0)
        swap = swap - jnp.where(jnp.logical_not(upper) & (column == row - CORR), 1.0, 0.0)
        swap = swap.astype(jnp.bfloat16)
        pieces = [own[at : at + part] for at in range(0, own.shape[0], part)]
        turned = [jnp.dot(swap, p, preferred_element_type=jnp.float32) for p in pieces]
        left[:row_count] = jnp.transpose(own.astype(jnp.float32)).astype(jnp.bfloat16)
        left[row_count:] = jnp.transpose(jnp.concatenate(turned, axis=0)).astype(jnp.bfloat16)

    columns = pl.ds(pl.multiple_of(step * tile, tile), tile)
    right = jnp.concatenate([r[:, columns] for r in blocks], axis=0)
    summed = jnp.dot(left[...], right, preferred_element_type=jnp.float32)
    if before:
        summed = summed + before[0][:, columns]
    if scale is None:
        out_ref[:, columns] = summed
    else:
        summed = summed * scale
        out_ref[0, 0] = summed[:row_count].astype(jnp.bfloat16)
        out_ref[0, 1] = summed[row_count:].astype(jnp.bfloat16)


def correlate(position, blocks, row_count, before=(), scale=None):
    signals = blocks[0].shape[1]
    depth = sum(b.shape[0] for b in blocks)
    tile = 1024
    whole = pl.BlockSpec(memory_space=pltpu.VMEM)
    if scale is None:
        out_spec = whole
        out_shape = jax.ShapeDtypeStruct((2 * row_count, signals), jnp.float32)
    else:
        out_spec = pl.BlockSpec((1, 2, row_count, tile), lambda g, p: (0, 0, 0, g))
        out_shape = jax.ShapeDtypeStruct((1, 2, row_count, signals), jnp.bfloat16)
    return pl.pallas_call(
        functools.partial(correlate_kernel, scale, len(blocks), tile),
        grid_spec=pltpu.PrefetchScalarGridSpec(
            num_scalar_prefetch=1,
            grid=(signals // tile,),
            in_specs=[whole] * (len(blocks) + len(before)),
            out_specs=out_spec,
            scratch_shapes=[pltpu.VMEM((2 * row_count, depth), jnp.bfloat16)],
        ),
        out_shape=out_shape,
        compiler_params=pltpu.CompilerParams(vmem_limit_bytes=VMEM_LIMIT),
        cost_estimate=pl.CostEstimate(
            flops=4 * row_count * signals * depth,
            bytes_accessed=2 * signals * depth + 8 * row_count * signals,
            transcendentals=0,
        ),
    )(position, *blocks, *before)


def from_slice(value, dx, dy):
    bands, slices = lax.axis_size("band"), lax.axis_size("tslice")
    along = slices // 2
    pairs = []
    for band in range(bands):
        way = -dx if band % 2 else dx
        for target in range(slices):
            source = ((target // 2 + way) % along) * 2 + (target % 2 + dy) % 2
            pairs.append((band * slices + source, band * slices + target))
    return lax.ppermute(value, ("band", "tslice"), pairs)


def gather_and_correlate(own, position, row_count, scale):
    take = from_slice
    right, other = take(own, 1, 0), take(own, 0, 1)
    own, summed = lax.optimization_barrier((own, correlate(position, [own], row_count)))
    left = take(own, -1, 0)
    summed = correlate(position, [right, other, left], row_count, [summed])
    right_other, left_other, far = take(right, 0, 1), take(other, -1, 0), take(right, 1, 0)
    right_other, summed = lax.optimization_barrier((right_other, summed))
    cut = own.shape[0] * 3 // 4
    last = [take(right_other[:cut], 1, 0), take(far[cut:], 0, 1)]
    summed = correlate(position, [right_other, left_other, far], row_count, [summed])
    return correlate(position, last, row_count, [summed], scale)


def on_device(voltages, taper, input_of, band_start):
    length = 2 * CHANNELS
    bands = lax.axis_size("band")
    slices = lax.axis_size("tslice")
    frames = voltages.shape[1] // length
    signals = input_of.shape[0]
    position = lax.axis_index("tslice")
    tail = voltages[:, (frames - TAPS + 1) * length :]
    before = lax.ppermute(tail, "tslice", [(s, s + 1) for s in range(slices - 1)])
    basis = jnp.asarray(make_basis(bands, length))
    half = frames // 2
    transform = functools.partial(picked_spectra, voltages, taper, basis, band_start)
    later = transform(tuple(range(half, frames)))
    spectra = transform(tuple(range(half)), before, later)
    turned = lax.all_to_all(spectra, "band", split_axis=0, concat_axis=0, tiled=True)
    own = order_signals(turned, input_of)
    position = position.astype(jnp.int32).reshape(1)
    scale = 1.0 / (CORR * frames * slices)
    return gather_and_correlate(own, position, signals // slices, scale)


def solution(mesh):
    return jax.shard_map(
        on_device,
        mesh=mesh,
        in_specs=(P("band", "tslice"), P(), P(), P()),
        out_specs=P("band", None, "tslice", None),
        check_vma=False,
    )
```

```python
import functools

import jax
import jax.numpy as jnp
import numpy as np
from jax import lax
from jax.experimental import pallas as pl
from jax.experimental.pallas import tpu as pltpu
from jax.sharding import PartitionSpec as P

CHANNELS = 1024
TAPS = 4
CORR = 12
VMEM_LIMIT = 16 << 20


def make_basis(bands, length):
    half = length // 2
    index = np.arange(half, dtype=np.int64)
    m = (np.arange(CHANNELS, dtype=np.int64)[:, None] * index[None, :]) % length
    phases = np.float32(2.0 * np.pi / length) * m.astype(np.float32)
    stacked = np.stack([np.cos(phases), -np.sin(phases)], axis=0)
    stacked = stacked.reshape(2, bands, CHANNELS // bands // 2, 2, half)
    stacked = stacked.transpose(3, 1, 0, 2, 4).reshape(2, CHANNELS, half)
    return stacked.astype(jnp.bfloat16)


def spectra_kernel(group, span, start_ref, volt_ref, taper_ref, basis_ref, *refs):
    out_ref, folded = refs[-2:]
    before_ref, later_ref = refs[:2] if len(refs) == 4 else (None, None)
    sig_dev = volt_ref.shape[0]
    length = taper_ref.shape[1]
    half = length // 2
    bands = out_ref.shape[0]
    columns = sig_dev * len(span)
    ch_band = basis_ref.shape[1] // bands

    def frame(at, second):
        first = second * half
        if at < 0:
            first = first + (at + TAPS - 1) * length
            return before_ref[:, first : first + half].astype(jnp.float32)
        first = first + at * length
        return volt_ref[:, first : first + half].astype(jnp.float32)

    parts = [[], [], [], []]
    for at in span:
        halves = []
        for second in range(2):
            place = slice(second * half, (second + 1) * half)
            total = taper_ref[0:1, place] * frame(at - TAPS + 1, second)
            for tap in range(1, TAPS):
                total = total + taper_ref[tap : tap + 1, place] * frame(at + tap - TAPS + 1, second)
            halves.append(total.astype(jnp.bfloat16).astype(jnp.float32))
        for odd, value in enumerate((halves[0] + halves[1], halves[0] - halves[1])):
            main = value.astype(jnp.bfloat16)
            parts[2 * odd].append(main)
            parts[2 * odd + 1].append((value - main.astype(jnp.float32)).astype(jnp.bfloat16))
    for odd in range(2):
        rows = jnp.concatenate(parts[2 * odd] + parts[2 * odd + 1], axis=0)
        folded[odd] = jnp.transpose(rows)

    part = 8
    held = part * ch_band
    shape = (2 * CORR, 2 * held)
    row = lax.broadcasted_iota(jnp.int32, shape, 0)
    column = lax.broadcasted_iota(jnp.int32, shape, 1)
    imag = column % ch_band // (ch_band // 2)
    channel = 2 * (column % (ch_band // 2)) + column // held
    band_at = column % held // ch_band
    wanted = channel - row % CORR + jnp.where(imag == row // CORR, 0, -2 * CHANNELS)

    def bands_from(at, carry):
        first = pl.multiple_of(at * group * ch_band, group * ch_band)
        products = []
        for odd in range(2):
            both = jnp.dot(
                basis_ref[odd, pl.ds(first, group * ch_band), :],
                folded[odd],
                preferred_element_type=jnp.float32,
            )
            products.append((both[:, :columns] + both[:, columns:]).astype(jnp.bfloat16))
        for begin in range(0, group, part):
            picks = [
                jnp.where(
                    (band_at == band) & (wanted == start_ref[at * group + begin + band]), 1.0, 0.0
                )
                for band in range(part)
            ]
            picked = jnp.concatenate(picks, axis=0).astype(jnp.bfloat16)
            place = slice(begin * ch_band, (begin + part) * ch_band)
            source = jnp.concatenate([p[place] for p in products], axis=0)
            spectra = jnp.dot(picked, source, preferred_element_type=jnp.float32)
            for band in range(part):
                these = spectra[band * 2 * CORR : (band + 1) * 2 * CORR].astype(jnp.bfloat16)
                if later_ref is not None:
                    later = later_ref[at * group + begin + band]
                    these = jnp.concatenate([these, later], axis=1)
                out_ref[at * group + begin + band] = these
        return carry

    lax.fori_loop(0, bands // group, bands_from, 0, unroll=True)


def picked_spectra(voltages, taper, basis, band_start, span, before=None, later=None):
    bands = band_start.shape[0]
    sig_dev, samples = voltages.shape
    length = taper.shape[1]
    columns = sig_dev * len(span)
    wide = columns if later is None else columns + later.shape[2]
    beside = [] if later is None else [before, later]
    whole = pl.BlockSpec(memory_space=pltpu.VMEM)
    return pl.pallas_call(
        functools.partial(spectra_kernel, 32, span),
        in_specs=[pl.BlockSpec(memory_space=pltpu.SMEM)] + [whole] * (3 + len(beside)),
        out_specs=whole,
        scratch_shapes=[pltpu.VMEM((2, length // 2, 2 * columns), jnp.bfloat16)],
        out_shape=jax.ShapeDtypeStruct((bands, 2 * CORR, wide), jnp.bfloat16),
        compiler_params=pltpu.CompilerParams(vmem_limit_bytes=VMEM_LIMIT),
        cost_estimate=pl.CostEstimate(
            flops=2 * CHANNELS * length * 2 * columns,
            bytes_accessed=2 * CHANNELS * length + 4 * sig_dev * samples,
            transcendentals=0,
        ),
    )(band_start, voltages, taper, basis, *beside)


def order_kernel(turned_ref, input_ref, out_ref, lined):
    bands, values, columns = turned_ref.shape
    signals = out_ref.shape[1]
    sig_dev = signals // bands
    frames = columns // sig_dev
    per_tile = 128 // sig_dev

    def tile(at, carry):
        lane = lax.broadcasted_iota(jnp.int32, (values, 128), 1) // sig_dev
        blocks = [turned_ref[at * per_tile + k].astype(jnp.float32) for k in range(per_tile)]
        for frame in range(frames):
            half, place = frame // per_tile, frame % per_tile
            merged = None
            for k in range(per_tile):
                piece = blocks[k][:, half * 128 : (half + 1) * 128]
                shift = (k - place) * sig_dev % 128
                if shift:
                    piece = pltpu.roll(piece, shift, 1)
                merged = piece if merged is None else jnp.where(lane == k, piece, merged)
            lined[at, frame * values : (frame + 1) * values, :] = merged
        return carry

    lax.fori_loop(0, bands // per_tile, tile, 0, unroll=True)
    held = jnp.concatenate([lined[at].astype(jnp.bfloat16) for at in range(signals // 128)], axis=1)
    part = 512
    row = lax.broadcasted_iota(jnp.int32, (16, part), 0).astype(jnp.int16)
    one = jnp.ones((16, part), jnp.bfloat16)
    zero = jnp.zeros((16, part), jnp.bfloat16)
    for at in range(0, signals, part):
        wanted = jnp.broadcast_to(input_ref[:, at : at + part], (16, part)).astype(jnp.int16)
        chosen = jnp.concatenate(
            [jnp.where(row == wanted - first, one, zero) for first in range(0, signals, 16)], axis=0
        )
        out_ref[:, at : at + part] = jnp.dot(
            held, chosen, preferred_element_type=jnp.float32
        ).astype(jnp.bfloat16)


def order_signals(turned, input_of):
    bands, values, columns = turned.shape
    signals = input_of.shape[0]
    rows = values * columns * bands // signals
    return pl.pallas_call(
        order_kernel,
        in_specs=[pl.BlockSpec(memory_space=pltpu.VMEM)] * 2,
        out_specs=pl.BlockSpec(memory_space=pltpu.VMEM),
        out_shape=jax.ShapeDtypeStruct((rows, signals), jnp.bfloat16),
        scratch_shapes=[pltpu.VMEM((signals // 128, rows, 128), jnp.float32)],
        compiler_params=pltpu.CompilerParams(vmem_limit_bytes=VMEM_LIMIT),
        cost_estimate=pl.CostEstimate(
            flops=2 * rows * signals * signals,
            bytes_accessed=4 * rows * signals,
            transcendentals=0,
        ),
    )(turned, input_of.reshape(1, signals))


def correlate_kernel(scale, count, tile, position_ref, *refs):
    blocks, before, out_ref, left = refs[:count], refs[count:-2], refs[-2], refs[-1]
    row_count = left.shape[0] // 2
    values = 2 * CORR
    step = pl.program_id(0)

    @pl.when(step == 0)
    def _():
        first = pl.multiple_of(position_ref[0] * row_count, row_count)
        own = jnp.concatenate([r[:, pl.ds(first, row_count)] for r in blocks], axis=0)
        part = 192
        row = lax.broadcasted_iota(jnp.int32, (part, part), 0)
        column = lax.broadcasted_iota(jnp.int32, (part, part), 1)
        upper = row % values < CORR
        swap = jnp.where(upper & (column == row + CORR), 1.0, 0.0)
        swap = swap - jnp.where(jnp.logical_not(upper) & (column == row - CORR), 1.0, 0.0)
        swap = swap.astype(jnp.bfloat16)
        pieces = [own[at : at + part] for at in range(0, own.shape[0], part)]
        turned = [jnp.dot(swap, p, preferred_element_type=jnp.float32) for p in pieces]
        left[:row_count] = jnp.transpose(own.astype(jnp.float32)).astype(jnp.bfloat16)
        left[row_count:] = jnp.transpose(jnp.concatenate(turned, axis=0)).astype(jnp.bfloat16)

    columns = pl.ds(pl.multiple_of(step * tile, tile), tile)
    right = jnp.concatenate([r[:, columns] for r in blocks], axis=0)
    summed = jnp.dot(left[...], right, preferred_element_type=jnp.float32)
    if before:
        summed = summed + before[0][:, columns]
    if scale is None:
        out_ref[:, columns] = summed
    else:
        summed = summed * scale
        out_ref[0, 0] = summed[:row_count].astype(jnp.bfloat16)
        out_ref[0, 1] = summed[row_count:].astype(jnp.bfloat16)


def correlate(position, blocks, row_count, before=(), scale=None):
    signals = blocks[0].shape[1]
    depth = sum(b.shape[0] for b in blocks)
    tile = 1024
    whole = pl.BlockSpec(memory_space=pltpu.VMEM)
    if scale is None:
        out_spec = whole
        out_shape = jax.ShapeDtypeStruct((2 * row_count, signals), jnp.float32)
    else:
        out_spec = pl.BlockSpec((1, 2, row_count, tile), lambda g, p: (0, 0, 0, g))
        out_shape = jax.ShapeDtypeStruct((1, 2, row_count, signals), jnp.bfloat16)
    return pl.pallas_call(
        functools.partial(correlate_kernel, scale, len(blocks), tile),
        grid_spec=pltpu.PrefetchScalarGridSpec(
            num_scalar_prefetch=1,
            grid=(signals // tile,),
            in_specs=[whole] * (len(blocks) + len(before)),
            out_specs=out_spec,
            scratch_shapes=[pltpu.VMEM((2 * row_count, depth), jnp.bfloat16)],
        ),
        out_shape=out_shape,
        compiler_params=pltpu.CompilerParams(vmem_limit_bytes=VMEM_LIMIT),
        cost_estimate=pl.CostEstimate(
            flops=4 * row_count * signals * depth,
            bytes_accessed=2 * signals * depth + 8 * row_count * signals,
            transcendentals=0,
        ),
    )(position, *blocks, *before)


def from_slice(value, dx, dy):
    bands, slices = lax.axis_size("band"), lax.axis_size("tslice")
    along = slices // 2
    pairs = []
    for band in range(bands):
        way = -dx if band % 2 else dx
        for target in range(slices):
            source = ((target // 2 + way) % along) * 2 + (target % 2 + dy) % 2
            pairs.append((band * slices + source, band * slices + target))
    return lax.ppermute(value, ("band", "tslice"), pairs)


def gather_and_correlate(own, position, row_count, scale):
    take = from_slice
    right, other = take(own, 1, 0), take(own, 0, 1)
    own, summed = lax.optimization_barrier((own, correlate(position, [own], row_count)))
    left = take(own, -1, 0)
    summed = correlate(position, [right, other, left], row_count, [summed])
    right_other, left_other, far = take(right, 0, 1), take(other, -1, 0), take(right, 1, 0)
    right_other, summed = lax.optimization_barrier((right_other, summed))
    cut = own.shape[0] * 3 // 4
    last = [take(right_other[:cut], 1, 0), take(far[cut:], 0, 1)]
    summed = correlate(position, [right_other, left_other, far], row_count, [summed])
    return correlate(position, last, row_count, [summed], scale)


def on_device(voltages, taper, input_of, band_start):
    length = 2 * CHANNELS
    bands = lax.axis_size("band")
    slices = lax.axis_size("tslice")
    frames = voltages.shape[1] // length
    signals = input_of.shape[0]
    position = lax.axis_index("tslice")
    tail = voltages[:, (frames - TAPS + 1) * length :]
    before = lax.ppermute(tail, "tslice", [(s, s + 1) for s in range(slices - 1)])
    basis = jnp.asarray(make_basis(bands, length))
    half = frames // 2
    transform = functools.partial(picked_spectra, voltages, taper, basis, band_start)
    later = transform(tuple(range(half, frames)))
    spectra = transform(tuple(range(half)), before, later)
    turned = lax.all_to_all(spectra, "band", split_axis=0, concat_axis=0, tiled=True)
    own = order_signals(turned, input_of)
    position = position.astype(jnp.int32).reshape(1)
    scale = 1.0 / (CORR * frames * slices)
    return gather_and_correlate(own, position, signals // slices, scale)


def solution(mesh):
    return jax.shard_map(
        on_device,
        mesh=mesh,
        in_specs=(P("band", "tslice"), P(), P(), P()),
        out_specs=P("band", None, "tslice", None),
        check_vma=False,
    )
```
